256 devices in a mesh: row: 32 (over y, z_hi, core), col: 8 (over z_lo, x).
Axes of the slice: x: 4, y: 4, z: 8 (z_hi: 4, z_lo: 2; z = z_hi * 2 + z_lo), core: 2. Of those that a mesh axis runs over, the one named last changes fastest.
Arguments:
- pair_elems: bfloat16 [12288, 20000], P(('row', 'col')), may hold values from -0.5 to 0.5
- pair_bands: int32 [2, 12288], P(None, ('row', 'col')), may hold values from 0 to 255, as said below
- valence_energy: float32 [48], replicated, may hold values from -4 to -0.5
- conduction_energy: float32 [256], replicated, may hold values from 0.5 to 5
Outputs:
- polar_slab: float32 [2048, 20000], P('col', 'row')
The draws below stay inside these ranges and needn't reach their ends.
Inputs may be any that keep to these rules, and one draw needn't show every extreme that they name: `pair_bands`: each of the 12288 valence-conduction pairs appears exactly once; row 0 holds valence indices below 48, row 1 conduction indices below 256.
All inputs are finite; a program needn't handle non-finite values.
Results may differ from the reference program's by a relative error of at most 0.0024.
Values may be sent and summed in bfloat16 or wider, within the bound.
A program may use at most 128 MiB of HBM per device.

```python
import jax
import jax.numpy as jnp
from jax import lax

NG = 20000
NCOL = 2048
NCOND = 256
NPAIR = 12288
NVAL = 48


def draw_pair_bands(key, part):
    key = jax.random.fold_in(key, 7)
    shuffled = jax.random.permutation(key, NPAIR).astype(jnp.int32)
    return jnp.stack([shuffled // NCOND, shuffled % NCOND]).astype(jnp.int32)


def block_scale(key, shape, split, least, high):
    level, own = 1.0, jax.random.fold_in(key, 6)
    for position, blocks in split:
        steps = jnp.exp(jax.random.uniform(jax.random.fold_in(own, position), (blocks,), jnp.float32, least / len(split), high / len(split)))
        level = level * jnp.repeat(steps, shape[position] // blocks).reshape([-1 if axis == position else 1 for axis in range(len(shape))])
    return level


def normal_values(stream_key, extent, scale, reach, shards=(), dtype=jnp.bfloat16):
    values = jax.random.normal(stream_key, extent, jnp.float32) * scale
    if len(shards) > 0:
        values = block_scale(stream_key, extent, shards, -0.22, 0.18) * values
    return jnp.clip(values, min=-reach, max=reach).astype(dtype)


def setup_inputs(seed: int = 0) -> dict:
    splits = jax.random.split(jax.random.key(seed), 5)
    return {
        "pair_elems": normal_values(splits[0], (NPAIR, NG), (NPAIR ** -0.25), 0.5, ((0, 256),)),
        "pair_bands": draw_pair_bands(jax.random.fold_in(splits[4], 71), 0),
        "valence_energy": jnp.clip(jax.random.uniform(splits[2], (NVAL,), jnp.float32, -4.0, -0.5), -4.0, -0.5),
        "conduction_energy": jnp.clip(jax.random.uniform(splits[3], (NCOND,), jnp.float32, 0.5, 5.0), 0.5, 5.0),
    }


def reference(pair_elems, pair_bands, valence_energy, conduction_energy):
    weights = -4.0 / (conduction_energy[pair_bands[1]] - valence_energy[pair_bands[0]])
    weighted = (weights[:, None] * pair_elems[:, :NCOL].astype(jnp.float32)).astype(jnp.bfloat16)
    return jnp.dot(weighted.astype(jnp.float32).T, pair_elems.astype(jnp.float32), precision=lax.Precision.HIGHEST)
```

```python
import jax
import jax.numpy as jnp
from jax import lax
from jax.experimental import pallas as pl
from jax.experimental.pallas import tpu as pltpu
from jax.sharding import PartitionSpec as P

MESH = pl.DeviceIdType.MESH
NCOL = 2048
NG = 20000
GBLK = 625
QUART = 160
PAIRS = 48
NCH = 5
CH = 128
HALF = 1024


def body(pe, bands, val, con, out, tail, a_all, b_st, b_rc, c_acc, s_st, s_rc, f_st, gath,
         a_ss, a_rs, b_ss, b_rs, z_ss, z_rs, x_ss, x_rs, l_sem):
    row, col = lax.axis_index("row"), lax.axis_index("col")
    x, y, c = col % 4, row // 8, row % 2
    z = ((row // 2) % 4) * 2 + col // 4

    def dev(px, py, pz, pc):
        return (py * 8 + (pz // 2) * 2 + pc, (pz % 2) * 4 + px)

    def slot(px, py, pc):
        return pc * 16 + px * 4 + py

    def near(dx, dy):
        return dev((x + dx) % 4, (y + dy) % 4, z, c)

    offsets = [(dx, dy, dc) for dx, dy in ORDER for dc in range(2)] + [(0, 0, 1)]
    plane = [(lax.rem(x + dx, 4), lax.rem(y + dy, 4), lax.rem(c + dc, 2)) for dx, dy, dc in offsets]
    up, down = dev(x, y, (z + 1) % 8, c), dev(x, y, (z + 7) % 8, c)

    barrier = pltpu.get_barrier_semaphore()
    for px, py, pc in plane:
        pl.semaphore_signal(barrier, inc=1, device_id=dev(px, py, z, pc), device_id_type=MESH)
    for t in (up, down):
        pl.semaphore_signal(barrier, inc=1, device_id=t, device_id_type=MESH)

    eye = lax.broadcasted_iota(jnp.int32, (PAIRS, PAIRS), 0) == lax.broadcasted_iota(jnp.int32, (PAIRS, PAIRS), 1)
    bf = bands[...].astype(jnp.float32)

    def as_column(r):
        return jnp.sum(jnp.where(eye, jnp.broadcast_to(r, (PAIRS, PAIRS)), 0.0), axis=1, keepdims=True)

    def look_up(ids, table):
        n = table.shape[1]
        lanes = lax.broadcasted_iota(jnp.int32, (PAIRS, n), 1).astype(jnp.float32)
        return jnp.sum(jnp.where(ids == lanes, jnp.broadcast_to(table, (PAIRS, n)), 0.0), axis=1, keepdims=True)

    valence = look_up(as_column(bf[0:1]), val[...])
    conduct = look_up(as_column(bf[1:2]), con[...])
    weights = -4.0 / (conduct - valence)
    me = slot(x, y, c)
    mine = pl.multiple_of(me * PAIRS, 16)
    a_all[pl.ds(mine, PAIRS), :] = (weights * pe[:, :NCOL].astype(jnp.float32)).astype(jnp.bfloat16)

    pl.semaphore_wait(barrier, len(plane) + 2)

    index = {}

    def piece(px, py, cols):
        r = pl.multiple_of(slot(px, py, c) * PAIRS, 16)
        return a_all.at[pl.ds(r, PAIRS), pl.ds(cols[0], cols[1])]

    def a_copy(key, px, py, cols, target):
        i = index.setdefault(key, len(index))
        ref = piece(px, py, cols)
        return pltpu.make_async_remote_copy(src_ref=ref, dst_ref=ref, send_sem=a_ss.at[i], recv_sem=a_rs.at[i],
                                            device_id=target, device_id_type=MESH)

    sent = []

    def a_send(key, px, py, cols, target):
        cp = a_copy(key, px, py, cols, target)
        cp.start()
        sent.append(cp)

    def a_wait(key, px, py, cols):
        a_copy(key, px, py, cols, near(1, 0)).wait_recv()

    def at(h, d1, d2):
        dx, dy = (d1, d2) if h == 0 else (d2, d1)
        return (x + dx) % 4, (y + dy) % 4

    def to(h, d1, d2):
        px, py = at(h, d1, d2)
        return dev(px, py, z, c)

    full = {0: (0, 1024), 1: (1024, 1024)}
    part = {(h, s): (h * 1024 + (0 if s == 1 else 512), 512) for h in (0, 1) for s in (1, 3)}
    for h in (0, 1):
        for s in (1, 3):
            a_send(("p1", h, s), x, y, full[h], to(h, s, 0))
    for h in (0, 1):
        for s in (1, 3):
            a_send(("p2", h, 0, s), x, y, full[h], to(h, 0, s))

    tail[...] = jnp.zeros_like(tail)
    tail[:, 0:32] = pe[:, NG - 32:NG]
    lane = lax.broadcasted_iota(jnp.int32, (PAIRS, CH), 1)

    def source(tile):
        v = tail[...] if tile == NG // CH else pe[:, tile * CH:(tile + 1) * CH]
        return v.astype(jnp.float32)

    def stage(t):
        for pc in range(2):
            for px in range(4):
                for py in range(4):
                    acc = None
                    for zh in range(4):
                        start = (py * 8 + zh * 2 + pc) * GBLK + px * QUART + t * 32
                        tile, off = start // CH, start % CH
                        shift = (32 * zh - off) % CH
                        v = pltpu.roll(source(tile), shift, 1)
                        if off > 96 and tile < NG // CH:
                            v = jnp.where(lane < 32 * zh + CH - off, v, pltpu.roll(source(tile + 1), shift, 1))
                        acc = v if acc is None else jnp.where(lane < 32 * zh, acc, v)
                    b_st[t, slot(px, py, pc)] = acc.astype(jnp.bfloat16)

    def b_send(t):
        for px, py, pc in plane:
            pltpu.make_async_remote_copy(
                src_ref=b_st.at[t, slot(px, py, pc)], dst_ref=b_rc.at[t, pl.ds(mine, PAIRS)],
                send_sem=b_ss.at[t], recv_sem=b_rs.at[t], device_id=dev(px, py, z, pc), device_id_type=MESH).start()

    def b_done(t):
        return pltpu.make_async_remote_copy(
            src_ref=b_rc.at[t, pl.ds(0, 31 * PAIRS)], dst_ref=b_rc.at[t, pl.ds(0, 31 * PAIRS)],
            send_sem=b_ss.at[t], recv_sem=b_rs.at[t], device_id=near(1, 0), device_id_type=MESH)

    for t in range(NCH):
        stage(t)
        b_rc[t, pl.ds(mine, PAIRS)] = b_st[t, me]

    for s in (1, 3):
        for h in (0, 1):
            px, py = at(h, -s, 0)
            a_wait(("p1", h, s), px, py, full[h])
            a_send(("f1", h, s), px, py, part[h, s], to(h, s, 0))
            for u in (1, 3):
                a_send(("p2", h, s, u), px, py, full[h], to(h, 0, u))
    for s in (1, 3):
        for h in (0, 1):
            px, py = at(h, 2, 0)
            a_wait(("f1", h, s), px, py, part[h, s])
            for u in (1, 3):
                a_send(("p2q", h, s, u), px, py, part[h, s], to(h, 0, u))
    for q in (0, 1, 3):
        for u in (1, 3):
            for h in (0, 1):
                px, py = at(h, -q, -u)
                a_wait(("p2", h, q, u), px, py, full[h])
                a_send(("f2", h, q, u), px, py, part[h, u], to(h, 0, u))
    for u in (1, 3):
        for s in (1, 3):
            for h in (0, 1):
                px, py = at(h, 2, -u)
                a_wait(("p2q", h, s, u), px, py, part[h, s])
                if s == u:
                    a_send(("f2", h, 2, u), px, py, part[h, u], to(h, 0, u))
    for t in range(NCH):
        b_send(t)
    for q in (0, 1, 3, 2):
        for u in (1, 3):
            for h in (0, 1):
                px, py = at(h, -q, 2)
                a_wait(("f2", h, q, u), px, py, part[h, u])
    own = pl.multiple_of(c * 16 * PAIRS, 16)
    i = len(index)
    theirs = a_all.at[pl.ds(own, 16 * PAIRS)]
    sib = pltpu.make_async_remote_copy(src_ref=theirs, dst_ref=theirs, send_sem=a_ss.at[i], recv_sem=a_rs.at[i],
                                       device_id=dev(x, y, z, 1 - c), device_id_type=MESH)
    sib.start()
    sent.append(sib)
    sib.wait_recv()

    def multiply(t):
        bt = b_rc[t].T

        def columns(n, carry):
            w = pl.ds(pl.multiple_of(n * 512, 512), 512)
            c_acc[t, :, w] = jnp.dot(bt, a_all[:, w], preferred_element_type=jnp.float32)
            return carry

        lax.fori_loop(0, NCOL // 512, columns, 0)

    def z_copy(t, d, s):
        rows = pl.ds(16 * d, 16) if s == 0 else pl.ds(0, 32)
        return pltpu.make_async_remote_copy(
            src_ref=s_st.at[t, d, s, rows], dst_ref=s_rc.at[t, d, s, rows], send_sem=z_ss.at[t, d, s],
            recv_sem=z_rs.at[t, d, s], device_id=(down, up)[d], device_id_type=MESH)

    def own_part(t, dz):
        goal = (z + dz) % 8
        return c_acc[t, pl.ds(pl.multiple_of((goal // 2) * 32, 32), 32),
                     pl.ds(pl.multiple_of((goal % 2) * HALF, HALF), HALF)]

    def x_copy(t, dx):
        px = (x + dx) % 4
        return pltpu.make_async_remote_copy(
            src_ref=f_st.at[t, :, pl.ds(pl.multiple_of(px * 256, 256), 256)],
            dst_ref=gath.at[pl.ds(pl.multiple_of(x * QUART + t * 32, 32), 32)],
            send_sem=x_ss.at[t], recv_sem=x_rs.at[t], device_id=dev(px, y, z, c), device_id_type=MESH)

    def x_done(t):
        return pltpu.make_async_remote_copy(
            src_ref=gath.at[pl.ds(0, 96)], dst_ref=gath.at[pl.ds(0, 96)],
            send_sem=x_ss.at[t], recv_sem=x_rs.at[t], device_id=near(1, 0), device_id_type=MESH)

    def reduce_step(t, s):
        if s == 0:
            v = own_part(t, 4).astype(jnp.bfloat16)
            for d in (0, 1):
                s_st[t, d, 0, 16 * d:16 * d + 16] = v[16 * d:16 * d + 16]
                z_copy(t, d, 0).start()
        elif s < 4:
            for d in (0, 1):
                z_copy(t, d, s - 1).wait_recv()
                v = own_part(t, (s - 4) if d == 0 else (4 - s))
                if s == 1:
                    got = s_rc[t, d, 0, 16 * d:16 * d + 16].astype(jnp.float32)
                    s_st[t, d, 1, 16 * d:16 * d + 16] = (v[16 * d:16 * d + 16] + got).astype(jnp.bfloat16)
                    e = 1 - d
                    s_st[t, d, 1, 16 * e:16 * e + 16] = v[16 * e:16 * e + 16].astype(jnp.bfloat16)
                else:
                    s_st[t, d, s] = (v + s_rc[t, d, s - 1].astype(jnp.float32)).astype(jnp.bfloat16)
                z_copy(t, d, s).start()
        else:
            for d in (0, 1):
                z_copy(t, d, 3).wait_recv()
            f_st[t] = own_part(t, 0) + s_rc[t, 0, 3].astype(jnp.float32) + s_rc[t, 1, 3].astype(jnp.float32)
            for dx in (2, 1, 3):
                x_copy(t, dx).start()
            gath[pl.ds(pl.multiple_of(x * QUART + t * 32, 32), 32)] = f_st[t, :, pl.ds(pl.multiple_of(x * 256, 256), 256)]

    for k in range(NCH + 4):
        for s in (4, 3, 2, 1):
            if 0 <= k - s < NCH:
                reduce_step(k - s, s)
        if k < NCH:
            b_done(k).wait_recv()
            multiply(k)
            reduce_step(k, 0)

    for t in range(NCH):
        x_done(t).wait_recv()
    out[...] = gath[...].T[:, :GBLK]

    for cp in sent:
        cp.wait_send()
    for t in range(NCH):
        b_done(t).wait_send()
        x_done(t).wait_send()
        for d in (0, 1):
            for s in range(4):
                z_copy(t, d, s).wait_send()


ORDER = [(2, 2), (1, 2), (2, 1), (3, 2), (2, 3), (2, 0), (0, 2), (1, 1), (3, 3), (1, 3), (3, 1), (1, 0), (3, 0), (0, 1), (0, 3)]
N_A = 45


def shards(pair_elems, pair_bands, valence_energy, conduction_energy):
    vm = pl.BlockSpec(memory_space=pltpu.VMEM)
    bf, f32, dma = jnp.bfloat16, jnp.float32, pltpu.SemaphoreType.DMA
    return pl.pallas_call(
        body,
        out_shape=jax.ShapeDtypeStruct((256, GBLK), f32),
        in_specs=[vm] * 4,
        out_specs=vm,
        scratch_shapes=[
            pltpu.VMEM((PAIRS, CH), bf),
            pltpu.VMEM((32 * PAIRS, NCOL), bf),
            pltpu.VMEM((NCH, 32, PAIRS, CH), bf),
            pltpu.VMEM((NCH, 32 * PAIRS, CH), bf),
            pltpu.VMEM((NCH, CH, NCOL), f32),
            pltpu.VMEM((NCH, 2, 4, 32, HALF), bf),
            pltpu.VMEM((NCH, 2, 4, 32, HALF), bf),
            pltpu.VMEM((NCH, 32, HALF), f32),
            pltpu.VMEM((4 * QUART, 256), f32),
            dma((N_A,)), dma((N_A,)), dma((NCH,)), dma((NCH,)),
            dma((NCH, 2, 4)), dma((NCH, 2, 4)), dma((NCH,)), dma((NCH,)), dma((1,)),
        ],
        compiler_params=pltpu.CompilerParams(collective_id=0, has_side_effects=True, vmem_limit_bytes=48 * 2**20),
        cost_estimate=pl.CostEstimate(flops=2 * 1536 * 2048 * 640, bytes_accessed=3 * 2**20, transcendentals=0),
        name="polar",
    )(pair_elems, pair_bands, valence_energy.reshape(1, -1), conduction_energy.reshape(1, -1))


def solution(mesh):
    placed = (P(("row", "col"), None), P(None, ("row", "col")), P(), P())
    return jax.shard_map(shards, mesh=mesh, in_specs=placed, out_specs=P("col", "row"), check_vma=False)
```

```python
import jax
import jax.numpy as jnp
from jax import lax
from jax.experimental import pallas as pl
from jax.experimental.pallas import tpu as pltpu
from jax.sharding import PartitionSpec as P

MESH = pl.DeviceIdType.MESH
NCOL = 2048
NG = 20000
GBLK = 625
QUART = 160
PAIRS = 48
NCH = 5
CH = 128
HALF = 1024


def body(pe_hbm, bands_hbm, val_hbm, con_hbm, out, pe, slab, bands, val, con, tail, a_all, b_st, b_rc, b_t, c_acc, s_st, s_rc, f_st, gath,
         a_ss, a_rs, b_ss, b_rs, z_ss, z_rs, x_ss, x_rs, c_ss, c_rs, l_sem):
    row, col = lax.axis_index("row"), lax.axis_index("col")
    x, y, c = col % 4, row // 8, row % 2
    z = ((row // 2) % 4) * 2 + col // 4

    def dev(px, py, pz, pc):
        return (py * 8 + (pz // 2) * 2 + pc, (pz % 2) * 4 + px)

    def slot(px, py, pc):
        return pc * 16 + px * 4 + py

    def near(dx, dy):
        return dev((x + dx) % 4, (y + dy) % 4, z, c)

    offsets = [(dx, dy, dc) for dx, dy in ORDER for dc in range(2)] + [(0, 0, 1)]
    plane = [(lax.rem(x + dx, 4), lax.rem(y + dy, 4), lax.rem(c + dc, 2)) for dx, dy, dc in offsets]
    up, down = dev(x, y, (z + 1) % 8, c), dev(x, y, (z + 7) % 8, c)

    barrier = pltpu.get_barrier_semaphore()
    for px, py, pc in plane:
        pl.semaphore_signal(barrier, inc=1, device_id=dev(px, py, z, pc), device_id_type=MESH)
    for t in (up, down):
        pl.semaphore_signal(barrier, inc=1, device_id=t, device_id_type=MESH)

    loads = [pltpu.make_async_copy(src, dst, l_sem.at[i]) for i, (src, dst) in enumerate([
        (bands_hbm, bands), (val_hbm, val), (con_hbm, con), (pe_hbm.at[:, pl.ds(0, NCOL)], slab), (pe_hbm, pe)])]
    for cp in loads:
        cp.start()
    for cp in loads[:3]:
        cp.wait()

    eye = lax.broadcasted_iota(jnp.int32, (PAIRS, PAIRS), 0) == lax.broadcasted_iota(jnp.int32, (PAIRS, PAIRS), 1)
    bf = bands[...].astype(jnp.float32)

    def as_column(r):
        return jnp.sum(jnp.where(eye, jnp.broadcast_to(r, (PAIRS, PAIRS)), 0.0), axis=1, keepdims=True)

    def look_up(ids, table):
        n = table.shape[1]
        lanes = lax.broadcasted_iota(jnp.int32, (PAIRS, n), 1).astype(jnp.float32)
        return jnp.sum(jnp.where(ids == lanes, jnp.broadcast_to(table, (PAIRS, n)), 0.0), axis=1, keepdims=True)

    valence = look_up(as_column(bf[0:1]), val[...])
    conduct = look_up(as_column(bf[1:2]), con[...])
    weights = -4.0 / (conduct - valence)
    me = slot(x, y, c)
    mine = pl.multiple_of(me * PAIRS, 16)
    loads[3].wait()
    a_all[pl.ds(mine, PAIRS), :] = (weights * slab[...].astype(jnp.float32)).astype(jnp.bfloat16)

    pl.semaphore_wait(barrier, len(plane) + 2)

    index = {}

    def piece(px, py, cols):
        r = pl.multiple_of(slot(px, py, c) * PAIRS, 16)
        return a_all.at[pl.ds(r, PAIRS), pl.ds(cols[0], cols[1])]

    def a_copy(key, px, py, cols, target):
        i = index.setdefault(key, len(index))
        ref = piece(px, py, cols)
        return pltpu.make_async_remote_copy(src_ref=ref, dst_ref=ref, send_sem=a_ss.at[i], recv_sem=a_rs.at[i],
                                            device_id=target, device_id_type=MESH)

    sent = []

    def a_send(key, px, py, cols, target):
        cp = a_copy(key, px, py, cols, target)
        cp.start()
        sent.append(cp)

    def a_wait(key, px, py, cols):
        a_copy(key, px, py, cols, near(1, 0)).wait_recv()

    def at(h, d1, d2):
        dx, dy = (d1, d2) if h == 0 else (d2, d1)
        return (x + dx) % 4, (y + dy) % 4

    def to(h, d1, d2):
        px, py = at(h, d1, d2)
        return dev(px, py, z, c)

    def core_copy(px, py, h):
        ref = piece(px, py, full[h])
        return pltpu.make_async_remote_copy(src_ref=ref, dst_ref=ref, send_sem=c_ss.at[0], recv_sem=c_rs.at[0],
                                            device_id=dev(x, y, z, 1 - c), device_id_type=MESH)

    full = {0: (0, 1024), 1: (1024, 1024)}
    part = {(h, s): (h * 1024 + (0 if s == 1 else 512), 512) for h in (0, 1) for s in (1, 3)}
    for h in (0, 1):
        for s in (1, 3):
            a_send(("p1", h, s), x, y, full[h], to(h, s, 0))
    for h in (0, 1):
        for s in (1, 3):
            a_send(("p2", h, 0, s), x, y, full[h], to(h, 0, s))
    for h in (0, 1):
        core_copy(x, y, h).start()

    loads[4].wait()
    tail[...] = jnp.zeros_like(tail)
    tail[:, 0:32] = pe[:, NG - 32:NG]
    lane = lax.broadcasted_iota(jnp.int32, (PAIRS, CH), 1)

    def source(tile):
        v = tail[...] if tile == NG // CH else pe[:, tile * CH:(tile + 1) * CH]
        return v.astype(jnp.float32)

    def stage(t):
        for pc in range(2):
            for px in range(4):
                for py in range(4):
                    acc = None
                    for zh in range(4):
                        start = (py * 8 + zh * 2 + pc) * GBLK + px * QUART + t * 32
                        tile, off = start // CH, start % CH
                        shift = (32 * zh - off) % CH
                        v = pltpu.roll(source(tile), shift, 1)
                        if off > 96 and tile < NG // CH:
                            v = jnp.where(lane < 32 * zh + CH - off, v, pltpu.roll(source(tile + 1), shift, 1))
                        acc = v if acc is None else jnp.where(lane < 32 * zh, acc, v)
                    b_st[t, slot(px, py, pc)] = acc.astype(jnp.bfloat16)

    def b_send(t):
        for px, py, pc in plane:
            pltpu.make_async_remote_copy(
                src_ref=b_st.at[t, slot(px, py, pc)], dst_ref=b_rc.at[t, pl.ds(mine, PAIRS)],
                send_sem=b_ss.at[t], recv_sem=b_rs.at[t], device_id=dev(px, py, z, pc), device_id_type=MESH).start()

    def b_done(t):
        return pltpu.make_async_remote_copy(
            src_ref=b_rc.at[t, pl.ds(0, 31 * PAIRS)], dst_ref=b_rc.at[t, pl.ds(0, 31 * PAIRS)],
            send_sem=b_ss.at[t], recv_sem=b_rs.at[t], device_id=near(1, 0), device_id_type=MESH)

    for t in range(NCH):
        stage(t)
        b_rc[t, pl.ds(mine, PAIRS)] = b_st[t, me]

    for s in (1, 3):
        for h in (0, 1):
            px, py = at(h, -s, 0)
            a_wait(("p1", h, s), px, py, full[h])
            a_send(("f1", h, s), px, py, part[h, s], to(h, s, 0))
            for u in (1, 3):
                a_send(("p2", h, s, u), px, py, full[h], to(h, 0, u))
            core_copy(px, py, h).start()
    for s in (1, 3):
        for h in (0, 1):
            px, py = at(h, 2, 0)
            a_wait(("f1", h, s), px, py, part[h, s])
            for u in (1, 3):
                a_send(("p2q", h, s, u), px, py, part[h, s], to(h, 0, u))
            if s == 3:
                core_copy(px, py, h).start()
    for q in (0, 1, 3):
        for u in (1, 3):
            for h in (0, 1):
                px, py = at(h, -q, -u)
                a_wait(("p2", h, q, u), px, py, full[h])
                a_send(("f2", h, q, u), px, py, part[h, u], to(h, 0, u))
                core_copy(px, py, h).start()
    for u in (1, 3):
        for s in (1, 3):
            for h in (0, 1):
                px, py = at(h, 2, -u)
                a_wait(("p2q", h, s, u), px, py, part[h, s])
                if s == u:
                    a_send(("f2", h, 2, u), px, py, part[h, u], to(h, 0, u))
                if s == 3:
                    core_copy(px, py, h).start()
    for t in range(WIN):
        b_send(t)
    for q in (0, 1, 3, 2):
        for u in (1, 3):
            for h in (0, 1):
                px, py = at(h, -q, 2)
                a_wait(("f2", h, q, u), px, py, part[h, u])
                if u == 3:
                    core_copy(px, py, h).start()
    own = pl.multiple_of(c * 16 * PAIRS, 16)
    theirs = a_all.at[pl.ds(pl.multiple_of((1 - c) * 16 * PAIRS, 16), 16 * PAIRS)]
    ours = a_all.at[pl.ds(own, 16 * PAIRS)]
    core_done = pltpu.make_async_remote_copy(src_ref=ours, dst_ref=theirs, send_sem=c_ss.at[0], recv_sem=c_rs.at[0],
                                             device_id=dev(x, y, z, 1 - c), device_id_type=MESH)
    core_done.wait_recv()

    def multiply(t, n):
        if n == 0:
            b_t[t] = b_rc[t].T
        w = slice(n * 512, n * 512 + 512)
        c_acc[t, :, w] = jnp.dot(b_t[t], a_all[:, w], preferred_element_type=jnp.float32)

    UR = 32 // SPLIT

    def z_copy(t, h, d, s):
        cols = pl.ds(512 * d, 512) if s == 0 else pl.ds(0, HALF)
        ref = (t, h, d, s, pl.ds(0, UR), cols)
        return pltpu.make_async_remote_copy(
            src_ref=s_st.at[ref], dst_ref=s_rc.at[ref], send_sem=z_ss.at[t, h, d, s],
            recv_sem=z_rs.at[t, h, d, s], device_id=(down, up)[d], device_id_type=MESH)

    def own_part(t, h, dz):
        goal = (z + dz) % 8
        return c_acc[t, pl.ds(pl.multiple_of((goal // 2) * 32 + h * UR, UR), UR),
                     pl.ds(pl.multiple_of((goal % 2) * HALF, HALF), HALF)]

    def x_copy(t, h, dx):
        px = (x + dx) % 4
        return pltpu.make_async_remote_copy(
            src_ref=f_st.at[t, pl.ds(h * UR, UR), pl.ds(pl.multiple_of(px * 256, 256), 256)],
            dst_ref=gath.at[pl.ds(pl.multiple_of(x * QUART + t * 32 + h * UR, UR), UR)],
            send_sem=x_ss.at[t], recv_sem=x_rs.at[t], device_id=dev(px, y, z, c), device_id_type=MESH)

    def x_done(t):
        return pltpu.make_async_remote_copy(
            src_ref=gath.at[pl.ds(0, 96)], dst_ref=gath.at[pl.ds(0, 96)],
            send_sem=x_ss.at[t], recv_sem=x_rs.at[t], device_id=near(1, 0), device_id_type=MESH)

    def reduce_step(t, h, s):
        if s == 0:
            v = own_part(t, h, 4).astype(jnp.bfloat16)
            for d in (0, 1):
                s_st[t, h, d, 0, :, 512 * d:512 * d + 512] = v[:, 512 * d:512 * d + 512]
                z_copy(t, h, d, 0).start()
        elif s < 4:
            for d in (0, 1):
                z_copy(t, h, d, s - 1).wait_recv()
                v = own_part(t, h, (s - 4) if d == 0 else (4 - s))
                if s == 1:
                    e = 1 - d
                    got = s_rc[t, h, d, 0, :, 512 * d:512 * d + 512].astype(jnp.float32)
                    s_st[t, h, d, 1, :, 512 * d:512 * d + 512] = (v[:, 512 * d:512 * d + 512] + got).astype(jnp.bfloat16)
                    s_st[t, h, d, 1, :, 512 * e:512 * e + 512] = v[:, 512 * e:512 * e + 512].astype(jnp.bfloat16)
                else:
                    s_st[t, h, d, s] = (v + s_rc[t, h, d, s - 1].astype(jnp.float32)).astype(jnp.bfloat16)
                z_copy(t, h, d, s).start()
        else:
            for d in (0, 1):
                z_copy(t, h, d, 3).wait_recv()
            total = own_part(t, h, 0) + s_rc[t, h, 0, 3].astype(jnp.float32) + s_rc[t, h, 1, 3].astype(jnp.float32)
            f_st[t, h * UR:h * UR + UR] = total
            for dx in (2, 1, 3):
                x_copy(t, h, dx).start()
            gath[pl.ds(pl.multiple_of(x * QUART + t * 32 + h * UR, UR), UR)] = (
                f_st[t, h * UR:h * UR + UR, pl.ds(pl.multiple_of(x * 256, 256), 256)])

    for op in plan():
        if op[0] == "b":
            k = op[1]
            b_done(k).wait_recv()
            if k + WIN < NCH:
                b_send(k + WIN)
        elif op[0] == "m":
            multiply(*op[1:])
        else:
            reduce_step(*op[1:])

    for t in range(NCH):
        x_done(t).wait_recv()
    out[...] = gath[...].T[:, :GBLK]

    for cp in sent:
        cp.wait_send()
    core_done.wait_send()
    for t in range(NCH):
        x_done(t).wait_send()
        for h in range(SPLIT):
            for d in (0, 1):
                for s in range(4):
                    z_copy(t, h, d, s).wait_send()
    for t in range(NCH):
        b_done(t).wait_send()


ORDER = [(2, 2), (1, 2), (2, 1), (3, 2), (2, 3), (2, 0), (0, 2), (1, 1), (3, 3), (1, 3), (3, 1), (1, 0), (3, 0), (0, 1), (0, 3)]
N_A = 44
WIN = 2
SPLIT = 2
B_GAP, WIRE, LATENCY, MULTIPLY, STEP, FINAL = 4.2, 1.43, 2.5, 0.45, 0.15, 0.3


def plan():
    came = {("b", k): k * B_GAP for k in range(NCH)}
    todo = [("b", k) for k in range(NCH)] + [("m", k, n) for k in range(NCH) for n in range(4)]
    todo += [("r", k, h, s) for k in range(NCH) for h in range(SPLIT) for s in range(5)]
    done, free, now, order = {}, 0.0, 0.0, []

    def ready(op):
        if op[0] == "b":
            return came[op] if all(("b", j) in done for j in range(op[1])) else None
        if op[0] == "m":
            need = [("b", op[1])] + [o for o in todo if o[0] == "m" and o < op]
            return max(done[o] for o in need) if all(o in done for o in need) else None
        return done.get(("m", op[1], 3)) if op[3] == 0 else came.get(("r",) + op[1:3] + (op[3] - 1,))

    def rank(op):
        return (0, op[1]) if op[0] == "b" else (1, -op[3], op[1], op[2]) if op[0] == "r" else (2,) + op[1:]

    while todo:
        times = [(ready(op), op) for op in todo]
        times = [(t, op) for t, op in times if t is not None]
        now = max(now, min(t for t, _ in times))
        op = min((o for t, o in times if t <= now), key=rank)
        now += 0.3 if op[0] == "b" else MULTIPLY if op[0] == "m" else FINAL if op[3] == 4 else STEP
        done[op] = now
        todo.remove(op)
        order.append(op)
        if op[0] == "r" and op[3] < 4:
            free = max(free, now) + WIRE / SPLIT * (0.5 if op[3] == 0 else 1)
            came[op] = free + LATENCY
    return order


def shards(pair_elems, pair_bands, valence_energy, conduction_energy):
    vm = pl.BlockSpec(memory_space=pltpu.VMEM)
    bf, f32, dma = jnp.bfloat16, jnp.float32, pltpu.SemaphoreType.DMA
    return pl.pallas_call(
        body,
        out_shape=jax.ShapeDtypeStruct((256, GBLK), f32),
        in_specs=[pl.BlockSpec(memory_space=pltpu.HBM)] * 4,
        out_specs=vm,
        scratch_shapes=[
            pltpu.VMEM((PAIRS, NG), bf),
            pltpu.VMEM((PAIRS, NCOL), bf),
            pltpu.VMEM((2, PAIRS), jnp.int32),
            pltpu.VMEM((1, 48), f32),
            pltpu.VMEM((1, 256), f32),
            pltpu.VMEM((PAIRS, CH), bf),
            pltpu.VMEM((32 * PAIRS, NCOL), bf),
            pltpu.VMEM((NCH, 32, PAIRS, CH), bf),
            pltpu.VMEM((NCH, 32 * PAIRS, CH), bf),
            pltpu.VMEM((NCH, CH, 32 * PAIRS), bf),
            pltpu.VMEM((NCH, CH, NCOL), f32),
            pltpu.VMEM((NCH, SPLIT, 2, 4, 32 // SPLIT, HALF), bf),
            pltpu.VMEM((NCH, SPLIT, 2, 4, 32 // SPLIT, HALF), bf),
            pltpu.VMEM((NCH, 32, HALF), f32),
            pltpu.VMEM((4 * QUART, 256), f32),
            dma((N_A,)), dma((N_A,)), dma((NCH,)), dma((NCH,)),
            dma((NCH, SPLIT, 2, 4)), dma((NCH, SPLIT, 2, 4)), dma((NCH,)), dma((NCH,)), dma((1,)), dma((1,)), dma((5,)),
        ],
        compiler_params=pltpu.CompilerParams(collective_id=0, has_side_effects=True, vmem_limit_bytes=48 * 2**20),
        cost_estimate=pl.CostEstimate(flops=2 * 1536 * 2048 * 640, bytes_accessed=3 * 2**20, transcendentals=0),
        name="polar",
    )(pair_elems, pair_bands, valence_energy.reshape(1, -1), conduction_energy.reshape(1, -1))


def solution(mesh):
    placed = (P(("row", "col"), None), P(None, ("row", "col")), P(), P())
    return jax.shard_map(shards, mesh=mesh, in_specs=placed, out_specs=P("col", "row"), check_vma=False)
```

```python
import jax
import jax.numpy as jnp
from jax import lax
from jax.experimental import pallas as pl
from jax.experimental.pallas import tpu as pltpu
from jax.sharding import PartitionSpec as P

MESH = pl.DeviceIdType.MESH
NCOL = 2048
NG = 20000
GBLK = 625
QUART = 160
PAIRS = 48
NCH = 5
CH = 128
HALF = 1024


def body(pe_hbm, bands_hbm, val_hbm, con_hbm, out, pe, slab, bands, val, con, tail, a_all, b_st, b_rc, b_t, c_acc, s_st, s_rc, f_st, gath,
         a_ss, a_rs, b_ss, b_rs, z_ss, z_rs, x_ss, x_rs, c_ss, c_rs, l_sem):
    row, col = lax.axis_index("row"), lax.axis_index("col")
    x, y, c = col % 4, row // 8, row % 2
    z = ((row // 2) % 4) * 2 + col // 4

    def dev(px, py, pz, pc):
        return (py * 8 + (pz // 2) * 2 + pc, (pz % 2) * 4 + px)

    def slot(px, py, pc):
        return pc * 16 + px * 4 + py

    def near(dx, dy):
        return dev((x + dx) % 4, (y + dy) % 4, z, c)

    offsets = [(dx, dy, dc) for dx, dy in ORDER for dc in range(2)] + [(0, 0, 1)]
    plane = [(lax.rem(x + dx, 4), lax.rem(y + dy, 4), lax.rem(c + dc, 2)) for dx, dy, dc in offsets]
    up, down = dev(x, y, (z + 1) % 8, c), dev(x, y, (z + 7) % 8, c)

    loads = [pltpu.make_async_copy(src, dst, l_sem.at[i]) for i, (src, dst) in enumerate([
        (bands_hbm, bands), (val_hbm, val), (con_hbm, con), (pe_hbm.at[:, pl.ds(0, NCOL)], slab), (pe_hbm, pe)])]
    for cp in loads:
        cp.start()
    barrier = pltpu.get_barrier_semaphore()
    for px, py, pc in plane:
        pl.semaphore_signal(barrier, inc=1, device_id=dev(px, py, z, pc), device_id_type=MESH)
    for t in (up, down):
        pl.semaphore_signal(barrier, inc=1, device_id=t, device_id_type=MESH)

    for cp in loads[:3]:
        cp.wait()

    eye = lax.broadcasted_iota(jnp.int32, (PAIRS, PAIRS), 0) == lax.broadcasted_iota(jnp.int32, (PAIRS, PAIRS), 1)
    bf = bands[...].astype(jnp.float32)

    def as_column(r):
        return jnp.sum(jnp.where(eye, jnp.broadcast_to(r, (PAIRS, PAIRS)), 0.0), axis=1, keepdims=True)

    def look_up(ids, table):
        n = table.shape[1]
        lanes = lax.broadcasted_iota(jnp.int32, (PAIRS, n), 1).astype(jnp.float32)
        return jnp.sum(jnp.where(ids == lanes, jnp.broadcast_to(table, (PAIRS, n)), 0.0), axis=1, keepdims=True)

    valence = look_up(as_column(bf[0:1]), val[...])
    conduct = look_up(as_column(bf[1:2]), con[...])
    weights = -4.0 / (conduct - valence)
    me = slot(x, y, c)
    mine = pl.multiple_of(me * PAIRS, 16)
    loads[3].wait()
    a_all[pl.ds(mine, PAIRS), :] = (weights * slab[...].astype(jnp.float32)).astype(jnp.bfloat16)

    pl.semaphore_wait(barrier, len(plane) + 2)

    index = {}

    def piece(px, py, cols):
        r = pl.multiple_of(slot(px, py, c) * PAIRS, 16)
        return a_all.at[pl.ds(r, PAIRS), pl.ds(cols[0], cols[1])]

    def a_copy(key, px, py, cols, target):
        i = index.setdefault(key, len(index))
        ref = piece(px, py, cols)
        return pltpu.make_async_remote_copy(src_ref=ref, dst_ref=ref, send_sem=a_ss.at[i], recv_sem=a_rs.at[i],
                                            device_id=target, device_id_type=MESH)

    sent = []

    def a_send(key, px, py, cols, target):
        cp = a_copy(key, px, py, cols, target)
        cp.start()
        sent.append(cp)

    def a_wait(key, px, py, cols):
        a_copy(key, px, py, cols, near(1, 0)).wait_recv()

    def at(h, d1, d2):
        dx, dy = (d1, d2) if h == 0 else (d2, d1)
        return (x + dx) % 4, (y + dy) % 4

    def to(h, d1, d2):
        px, py = at(h, d1, d2)
        return dev(px, py, z, c)

    def core_copy(px, py, h):
        ref = piece(px, py, full[h])
        return pltpu.make_async_remote_copy(src_ref=ref, dst_ref=ref, send_sem=c_ss.at[0], recv_sem=c_rs.at[0],
                                            device_id=dev(x, y, z, 1 - c), device_id_type=MESH)

    full = {0: (0, 1024), 1: (1024, 1024)}
    part = {(h, s): (h * 1024 + (0 if s == 1 else 512), 512) for h in (0, 1) for s in (1, 3)}
    for h in (0, 1):
        for s in (1, 3):
            a_send(("p1", h, s), x, y, full[h], to(h, s, 0))
    for h in (0, 1):
        for s in (1, 3):
            a_send(("p2", h, 0, s), x, y, full[h], to(h, 0, s))
    for h in (0, 1):
        core_copy(x, y, h).start()

    loads[4].wait()
    tail[...] = jnp.zeros_like(tail)
    tail[:, 0:32] = pe[:, NG - 32:NG]
    lane = lax.broadcasted_iota(jnp.int32, (PAIRS, CH), 1)

    def source(tile):
        v = tail[...] if tile == NG // CH else pe[:, tile * CH:(tile + 1) * CH]
        return v.astype(jnp.float32)

    def stage(t):
        for pc in range(2):
            for px in range(4):
                for py in range(4):
                    acc = None
                    for zh in range(4):
                        start = (py * 8 + zh * 2 + pc) * GBLK + px * QUART + t * 32
                        tile, off = start // CH, start % CH
                        shift = (32 * zh - off) % CH
                        v = pltpu.roll(source(tile), shift, 1)
                        if off > 96 and tile < NG // CH:
                            v = jnp.where(lane < 32 * zh + CH - off, v, pltpu.roll(source(tile + 1), shift, 1))
                        acc = v if acc is None else jnp.where(lane < 32 * zh, acc, v)
                    b_st[t, slot(px, py, pc)] = acc.astype(jnp.bfloat16)

    def b_send(t):
        for px, py, pc in plane:
            pltpu.make_async_remote_copy(
                src_ref=b_st.at[t, slot(px, py, pc)], dst_ref=b_rc.at[t, pl.ds(mine, PAIRS)],
                send_sem=b_ss.at[t], recv_sem=b_rs.at[t], device_id=dev(px, py, z, pc), device_id_type=MESH).start()

    def b_done(t):
        return pltpu.make_async_remote_copy(
            src_ref=b_rc.at[t, pl.ds(0, 31 * PAIRS)], dst_ref=b_rc.at[t, pl.ds(0, 31 * PAIRS)],
            send_sem=b_ss.at[t], recv_sem=b_rs.at[t], device_id=near(1, 0), device_id_type=MESH)

    for t in range(NCH):
        stage(t)
        b_rc[t, pl.ds(mine, PAIRS)] = b_st[t, me]

    for s in (1, 3):
        for h in (0, 1):
            px, py = at(h, -s, 0)
            a_wait(("p1", h, s), px, py, full[h])
            a_send(("f1", h, s), px, py, part[h, s], to(h, s, 0))
            for u in (1, 3):
                a_send(("p2", h, s, u), px, py, full[h], to(h, 0, u))
            core_copy(px, py, h).start()
    for s in (1, 3):
        for h in (0, 1):
            px, py = at(h, 2, 0)
            a_wait(("f1", h, s), px, py, part[h, s])
            for u in (1, 3):
                a_send(("p2q", h, s, u), px, py, part[h, s], to(h, 0, u))
            if s == 3:
                core_copy(px, py, h).start()
    for q in (0, 1, 3):
        for u in (1, 3):
            for h in (0, 1):
                px, py = at(h, -q, -u)
                a_wait(("p2", h, q, u), px, py, full[h])
                a_send(("f2", h, q, u), px, py, part[h, u], to(h, 0, u))
                core_copy(px, py, h).start()
    for u in (1, 3):
        for s in (1, 3):
            for h in (0, 1):
                px, py = at(h, 2, -u)
                a_wait(("p2q", h, s, u), px, py, part[h, s])
                if s == u:
                    a_send(("f2", h, 2, u), px, py, part[h, u], to(h, 0, u))
                if s == 3:
                    core_copy(px, py, h).start()
    for t in range(WIN):
        b_send(t)
    for q in (0, 1, 3, 2):
        for u in (1, 3):
            for h in (0, 1):
                px, py = at(h, -q, 2)
                a_wait(("f2", h, q, u), px, py, part[h, u])
                if u == 3:
                    core_copy(px, py, h).start()
    own = pl.multiple_of(c * 16 * PAIRS, 16)
    theirs = a_all.at[pl.ds(pl.multiple_of((1 - c) * 16 * PAIRS, 16), 16 * PAIRS)]
    ours = a_all.at[pl.ds(own, 16 * PAIRS)]
    core_done = pltpu.make_async_remote_copy(src_ref=ours, dst_ref=theirs, send_sem=c_ss.at[0], recv_sem=c_rs.at[0],
                                             device_id=dev(x, y, z, 1 - c), device_id_type=MESH)
    core_done.wait_recv()
    for cp in sent:
        cp.wait_send()
    core_done.wait_send()

    def multiply(t, n):
        if n == 0:
            b_t[t] = b_rc[t].T
        w = slice(n * 512, n * 512 + 512)
        c_acc[t, :, w] = jnp.dot(b_t[t], a_all[:, w], preferred_element_type=jnp.float32)

    UR = 32 // SPLIT

    def z_copy(t, h, d, s):
        cols = pl.ds(512 * d, 512) if s == 0 else pl.ds(0, HALF)
        ref = (t, h, d, s, pl.ds(0, UR), cols)
        return pltpu.make_async_remote_copy(
            src_ref=s_st.at[ref], dst_ref=s_rc.at[ref], send_sem=z_ss.at[t, h, d, s],
            recv_sem=z_rs.at[t, h, d, s], device_id=(down, up)[d], device_id_type=MESH)

    def own_part(t, h, dz):
        goal = (z + dz) % 8
        return c_acc[t, pl.ds(pl.multiple_of((goal // 2) * 32 + h * UR, UR), UR),
                     pl.ds(pl.multiple_of((goal % 2) * HALF, HALF), HALF)]

    def x_copy(t, h, dx):
        px = (x + dx) % 4
        return pltpu.make_async_remote_copy(
            src_ref=f_st.at[t, pl.ds(h * UR, UR), pl.ds(pl.multiple_of(px * 256, 256), 256)],
            dst_ref=gath.at[pl.ds(pl.multiple_of(x * QUART + t * 32 + h * UR, UR), UR)],
            send_sem=x_ss.at[t], recv_sem=x_rs.at[t], device_id=dev(px, y, z, c), device_id_type=MESH)

    def x_done(t):
        return pltpu.make_async_remote_copy(
            src_ref=gath.at[pl.ds(0, 96)], dst_ref=gath.at[pl.ds(0, 96)],
            send_sem=x_ss.at[t], recv_sem=x_rs.at[t], device_id=near(1, 0), device_id_type=MESH)

    def reduce_step(t, h, s):
        if s == 0:
            v = own_part(t, h, 4).astype(jnp.bfloat16)
            for d in (0, 1):
                s_st[t, h, d, 0, :, 512 * d:512 * d + 512] = v[:, 512 * d:512 * d + 512]
                z_copy(t, h, d, 0).start()
        elif s < 4:
            for d in (0, 1):
                z_copy(t, h, d, s - 1).wait_recv()
                v = own_part(t, h, (s - 4) if d == 0 else (4 - s))
                if s == 1:
                    e = 1 - d
                    got = s_rc[t, h, d, 0, :, 512 * d:512 * d + 512].astype(jnp.float32)
                    s_st[t, h, d, 1, :, 512 * d:512 * d + 512] = (v[:, 512 * d:512 * d + 512] + got).astype(jnp.bfloat16)
                    s_st[t, h, d, 1, :, 512 * e:512 * e + 512] = v[:, 512 * e:512 * e + 512].astype(jnp.bfloat16)
                else:
                    s_st[t, h, d, s] = (v + s_rc[t, h, d, s - 1].astype(jnp.float32)).astype(jnp.bfloat16)
                z_copy(t, h, d, s).start()
        else:
            for d in (0, 1):
                z_copy(t, h, d, 3).wait_recv()
            total = own_part(t, h, 0) + s_rc[t, h, 0, 3].astype(jnp.float32) + s_rc[t, h, 1, 3].astype(jnp.float32)
            f_st[t, h * UR:h * UR + UR] = total
            for dx in (2, 1, 3):
                x_copy(t, h, dx).start()
            gath[pl.ds(pl.multiple_of(x * QUART + t * 32 + h * UR, UR), UR)] = (
                f_st[t, h * UR:h * UR + UR, pl.ds(pl.multiple_of(x * 256, 256), 256)])

    ended = []

    def unit_sent(t, h):
        for d in (0, 1):
            for s in range(4):
                z_copy(t, h, d, s).wait_send()

    for op in plan():
        if op[0] == "b":
            k = op[1]
            b_done(k).wait_recv()
            if k > 0:
                b_done(k - 1).wait_send()
            if k + WIN < NCH:
                b_send(k + WIN)
        elif op[0] == "m":
            multiply(*op[1:])
        else:
            reduce_step(*op[1:])
            if op[3] == 4:
                ended.append(op[1:3])
                if len(ended) > 2:
                    unit_sent(*ended[-3])

    for t in range(NCH):
        x_done(t).wait_recv()
    out[...] = gath[...].T[:, :GBLK]

    for t, h in ended[-2:]:
        unit_sent(t, h)
    for t in range(NCH):
        x_done(t).wait_send()
    b_done(NCH - 1).wait_send()


ORDER = [(2, 2), (1, 2), (2, 1), (3, 2), (2, 3), (2, 0), (0, 2), (1, 1), (3, 3), (1, 3), (3, 1), (1, 0), (3, 0), (0, 1), (0, 3)]
N_A = 44
WIN = 2
SPLIT = 2
B_GAP, WIRE, LATENCY, MULTIPLY, STEP, FINAL = 4.2, 1.65, 2.5, 0.45, 0.15, 0.3


def plan():
    came = {("b", k): k * B_GAP for k in range(NCH)}
    todo = [("b", k) for k in range(NCH)] + [("m", k, n) for k in range(NCH) for n in range(4)]
    todo += [("r", k, h, s) for k in range(NCH) for h in range(SPLIT) for s in range(5)]
    done, free, now, order = {}, 0.0, 0.0, []

    def ready(op):
        if op[0] == "b":
            return came[op] if all(("b", j) in done for j in range(op[1])) else None
        if op[0] == "m":
            need = [("b", op[1])] + [o for o in todo if o[0] == "m" and o < op]
            return max(done[o] for o in need) if all(o in done for o in need) else None
        return done.get(("m", op[1], 3)) if op[3] == 0 else came.get(("r",) + op[1:3] + (op[3] - 1,))

    def rank(op):
        return (0, op[1]) if op[0] == "b" else (1, -op[3], op[1], op[2]) if op[0] == "r" else (2,) + op[1:]

    while todo:
        times = [(ready(op), op) for op in todo]
        times = [(t, op) for t, op in times if t is not None]
        now = max(now, min(t for t, _ in times))
        op = min((o for t, o in times if t <= now), key=rank)
        now += 0.3 if op[0] == "b" else MULTIPLY if op[0] == "m" else FINAL if op[3] == 4 else STEP
        done[op] = now
        todo.remove(op)
        order.append(op)
        if op[0] == "r" and op[3] < 4:
            free = max(free, now) + WIRE / SPLIT * (0.5 if op[3] == 0 else 1)
            came[op] = free + LATENCY
    return order


def shards(pair_elems, pair_bands, valence_energy, conduction_energy):
    vm = pl.BlockSpec(memory_space=pltpu.VMEM)
    bf, f32, dma = jnp.bfloat16, jnp.float32, pltpu.SemaphoreType.DMA
    return pl.pallas_call(
        body,
        out_shape=jax.ShapeDtypeStruct((256, GBLK), f32),
        in_specs=[pl.BlockSpec(memory_space=pltpu.HBM)] * 4,
        out_specs=vm,
        scratch_shapes=[
            pltpu.VMEM((PAIRS, NG), bf),
            pltpu.VMEM((PAIRS, NCOL), bf),
            pltpu.VMEM((2, PAIRS), jnp.int32),
            pltpu.VMEM((1, 48), f32),
            pltpu.VMEM((1, 256), f32),
            pltpu.VMEM((PAIRS, CH), bf),
            pltpu.VMEM((32 * PAIRS, NCOL), bf),
            pltpu.VMEM((NCH, 32, PAIRS, CH), bf),
            pltpu.VMEM((NCH, 32 * PAIRS, CH), bf),
            pltpu.VMEM((NCH, CH, 32 * PAIRS), bf),
            pltpu.VMEM((NCH, CH, NCOL), f32),
            pltpu.VMEM((NCH, SPLIT, 2, 4, 32 // SPLIT, HALF), bf),
            pltpu.VMEM((NCH, SPLIT, 2, 4, 32 // SPLIT, HALF), bf),
            pltpu.VMEM((NCH, 32, HALF), f32),
            pltpu.VMEM((4 * QUART, 256), f32),
            dma((N_A,)), dma((N_A,)), dma((NCH,)), dma((NCH,)),
            dma((NCH, SPLIT, 2, 4)), dma((NCH, SPLIT, 2, 4)), dma((NCH,)), dma((NCH,)), dma((1,)), dma((1,)), dma((5,)),
        ],
        compiler_params=pltpu.CompilerParams(collective_id=0, has_side_effects=True, vmem_limit_bytes=48 * 2**20),
        cost_estimate=pl.CostEstimate(flops=2 * 1536 * 2048 * 640, bytes_accessed=3 * 2**20, transcendentals=0),
        name="polar",
    )(pair_elems, pair_bands, valence_energy.reshape(1, -1), conduction_energy.reshape(1, -1))


def solution(mesh):
    placed = (P(("row", "col"), None), P(None, ("row", "col")), P(), P())
    return jax.shard_map(shards, mesh=mesh, in_specs=placed, out_specs=P("col", "row"), check_vma=False)
```
